128 devices in a mesh: pts: 32 (over y, z, core), lvl: 4 (over x).
Axes of the slice: x: 4, y: 4, z: 4, core: 2. Of those that a mesh axis runs over, the one named last changes fastest.
Arguments:
- signal: bfloat16 [16384, 2048], P(('pts', 'lvl')), may hold values from -6 to 6
- adjoint_in: bfloat16 [16384, 2048], P(('pts', 'lvl')), may hold values from -6 to 6
- factors: bfloat16 [9, 16384, 128, 64], P(None, ('pts', 'lvl')), may hold values from -0.5 to 0.5
- perms: int32 [2, 128], replicated, may hold values from 0 to 127, each once within a row
Outputs:
- forward_out: bfloat16 [16384, 2048], P(('pts', 'lvl'))
- adjoint_out: bfloat16 [16384, 2048], P(('pts', 'lvl'))
The draws below stay inside these ranges and needn't reach their ends.
Inputs may be any that keep to these rules, and one draw needn't show every extreme that they name: Each row of perms names every slot 0 to 127 once.
All inputs are finite; a program needn't handle non-finite values.
Results may differ from the reference program's by a relative error of at most 0.015.
Values may be sent and summed in bfloat16 or wider, within the bound.
No kernel may reach another device: no remote copies, remote signals or barrier semaphores. Data moves between devices by JAX's collectives and lax.ppermute only.
A program may use at most 192 MiB of HBM per device.

```python
import jax
import jax.numpy as jnp
from jax import lax

RANK = 64
RHS = 32
LEVELS = 9
BLK_DEV = 128
BLOCKS = 16384
N_PTS = 32
N_LVL = 4


def level_of(own_key, shape, cuts, smallest, largest):
    def one(axis_at, shards_of):
        steps = jax.random.uniform(jax.random.fold_in(jax.random.fold_in(own_key, 6), axis_at), (shards_of,), jnp.float32, smallest / len(cuts), largest / len(cuts))
        return jnp.repeat(jnp.exp(steps), shape[axis_at] // shards_of).reshape((-1,) + (1,) * (len(shape) - axis_at - 1))

    level = one(*cuts[0])
    for cut in cuts[1:]:
        level = level * one(*cut)
    return level


def scatter_about(own_key, dims, scale, bound, shards=(), kind=jnp.bfloat16):
    gain = level_of(own_key, dims, shards, -0.22, 0.18) if shards else 1.0
    array = jax.random.normal(own_key, dims, jnp.float32) * scale * gain
    return jnp.minimum(jnp.maximum(array, -bound), bound).astype(kind)


def setup_inputs(seed: int = 0) -> dict:
    splits = jax.random.split(jax.random.key(seed), 5)
    signal = scatter_about(splits[0], (BLOCKS, RHS * RANK), 1.0, 6.0, ((0, 128),))
    adjoint_in = scatter_about(splits[1], (BLOCKS, RHS * RANK), 1.0, 6.0, ((0, 128),))
    factors = scatter_about(splits[2], (LEVELS, BLOCKS, 2 * RANK, RANK), (2 * RANK) ** -0.5, 0.5, ((1, 128),))
    perms = jax.vmap(lambda own: jax.random.permutation(own, BLK_DEV))(jax.random.split(splits[3], 2)).reshape((2, BLK_DEV)).astype(jnp.int32)
    return dict(signal=signal, adjoint_in=adjoint_in, factors=factors, perms=perms)


pair_bits = (0, 1, 2, 1, 0)


def block_index(pnum, qnum, slot):
    full = (pnum * N_LVL + qnum) * BLK_DEV + slot
    return jnp.broadcast_to(full, (N_PTS, N_LVL, BLK_DEV)).reshape(-1).astype(jnp.int32)


def partner_maps(perms):
    pnum = jnp.arange(N_PTS, dtype=jnp.int32)[:, None, None]
    qnum = jnp.arange(N_LVL, dtype=jnp.int32)[None, :, None]
    slot = jnp.arange(BLK_DEV, dtype=jnp.int32)[None, None, :]
    width = BLK_DEV // N_LVL
    maps = [block_index(pnum, qnum, perms[0][None, None, :])]
    for bit in pair_bits:
        maps.append(block_index(jnp.bitwise_xor(pnum, 1 << bit), qnum, slot))
    for bit in range(2):
        maps.append(block_index(pnum, qnum, jnp.bitwise_xor(slot, (1 << bit) * width)))
    maps.append(block_index(pnum, qnum, perms[1][None, None, :]))
    return maps


def transpose_order(state):
    width = BLK_DEV // N_LVL
    shaped = state.reshape(N_PTS, N_LVL, N_LVL, width, RHS, RANK)
    return shaped.transpose(0, 2, 1, 3, 4, 5).reshape(BLOCKS, RHS, RANK)


def forward_level(state, weight, partner):
    statef = state.astype(jnp.float32)
    weightf = weight.astype(jnp.float32)
    mixed = jnp.einsum("brk,bkj->brj", statef, weightf[:, :RANK, :])
    mixed = mixed + jnp.einsum("brk,bkj->brj", statef[partner], weightf[:, RANK:, :])
    return mixed.astype(jnp.bfloat16)


def adjoint_level(state, weight, partner, sent):
    statef = state.astype(jnp.float32)
    weightf = weight.astype(jnp.float32)
    own = jnp.einsum("brj,bkj->brk", statef, weightf[:, :RANK, :])
    terms = jnp.einsum("brj,bkj->brk", statef, weightf[:, RANK:, :])
    if sent:
        terms = lax.optimization_barrier(terms.astype(jnp.bfloat16)).astype(jnp.float32)
    gathered = jnp.zeros_like(terms).at[partner].add(terms)
    return (own + gathered).astype(jnp.bfloat16)


def reference(signal, adjoint_in, factors, perms):
    maps = partner_maps(perms)
    state = signal.reshape(BLOCKS, RHS, RANK)
    for level in range(6):
        state = forward_level(state, factors[level], maps[level])
    state = transpose_order(state)
    for level in range(6, 9):
        state = forward_level(state, factors[level], maps[level])
    forward_out = state.reshape(BLOCKS, RHS * RANK)
    back = adjoint_in.reshape(BLOCKS, RHS, RANK)
    for level in (8, 7, 6):
        back = adjoint_level(back, factors[level], maps[level], False)
    back = transpose_order(back)
    for level in (5, 4, 3, 2, 1):
        back = adjoint_level(back, factors[level], maps[level], True)
    back = adjoint_level(back, factors[0], maps[0], False)
    return forward_out, back.reshape(BLOCKS, RHS * RANK)
```

```python
import functools

import jax
import jax.numpy as jnp
from jax import lax
from jax.experimental import pallas as pl
from jax.experimental.pallas import tpu as pltpu
from jax.sharding import PartitionSpec as P

f32, bf16 = jnp.float32, jnp.bfloat16
pair_bits = (0, 1, 2, 1, 0)
BLK, ROWS, LANES, RANK = 128, 16, 128, 64
CHUNKS, WIDTH = 4, 32
STATE = (BLK, ROWS, LANES)
PIECE = (WIDTH, ROWS, LANES)
NT = (((1,), (1,)), ((), ()))
NN = (((1,), (0,)), ((), ()))
HBM = pl.BlockSpec(memory_space=pl.ANY)
SMEM = pl.BlockSpec(memory_space=pltpu.SMEM)
DMA = pltpu.SemaphoreType.DMA


def low_half():
    return lax.broadcasted_iota(jnp.int32, (ROWS, LANES), 1) < RANK


def swap(x):
    return jnp.concatenate([x[:, RANK:], x[:, :RANK]], 1)


def forward_pair(low, first, second, factor):
    rows = []
    for own, other in (first, second):
        rows += [jnp.where(low, own, swap(other)), jnp.where(low, swap(own), other)]
    out = lax.dot_general(
        jnp.concatenate(rows, 0), factor.reshape(2 * RANK, LANES), NT, preferred_element_type=f32
    ).astype(bf16)
    return (
        jnp.where(low, out[0:16], swap(out[16:32])),
        jnp.where(low, swap(out[32:48]), out[48:64]),
    )


def adjoint_pair(low, first, second, factor):
    zero = jnp.zeros((ROWS, LANES), bf16)
    rows = [
        jnp.where(low, first, zero),
        jnp.where(low, swap(first), zero),
        jnp.where(low, zero, swap(second)),
        jnp.where(low, zero, second),
    ]
    out = lax.dot_general(
        jnp.concatenate(rows, 0), factor.reshape(2 * RANK, LANES), NN, preferred_element_type=f32
    )
    return (out[0:16], out[16:32]), (out[32:48], out[48:64])


def pack_own(low, parts):
    return jnp.where(low, parts[0], swap(parts[1]))


def pack_terms(low, parts):
    return jnp.where(low, swap(parts[0]), parts[1])


def fetch_factors(level, factors, hold, sem):
    copies = []
    for c in range(CHUNKS):
        part = pl.ds(c * WIDTH, WIDTH)
        copies.append(pltpu.make_async_copy(factors.at[level, part], hold.at[part], sem.at[c]))
        copies[-1].start()
    return copies


def fetch(source, hold, sem):
    copy = pltpu.make_async_copy(source, hold, sem)
    copy.start()
    return copy


def fetch_pieces(place, pieces, hold, sem):
    return [
        fetch(piece, hold.at[pl.ds((place ^ d) * WIDTH, WIDTH)], sem.at[d])
        for d, piece in enumerate(pieces)
    ]


def send_pieces(place, hold, pieces, sem):
    copies = [
        fetch(hold.at[pl.ds((place ^ d) * WIDTH, WIDTH)], piece, sem.at[d])
        for d, piece in enumerate(pieces)
    ]
    for copy in copies:
        copy.wait()


def to_blocks(flat, hold):
    for k in range(BLK // 16):
        part = slice(k * 16, k * 16 + 16)
        hold[part] = flat[part, :].reshape(16, ROWS, LANES)


def forward_blocks(copies, own, other, factor, out):
    low = low_half()
    for c in range(CHUNKS):
        copies[c].wait()
        for a in range(c * WIDTH, (c + 1) * WIDTH, 2):
            out[a], out[a + 1] = forward_pair(
                low, (own(a), other(a)), (own(a + 1), other(a + 1)), factor[a : a + 2]
            )


def adjoint_blocks(copies, state, factor, put):
    low = low_half()
    for c in range(CHUNKS):
        copies[c].wait()
        for a in range(c * WIDTH, (c + 1) * WIDTH, 2):
            pair = adjoint_pair(low, state(a), state(a + 1), factor[a : a + 2])
            for b in range(2):
                put(a + b, pack_own(low, pair[b]), pair[b])


def forward_head(perms, signal, factors, out_h, flat, hold, factor, out, fsem, sem):
    copy = fetch(signal, flat, sem.at[0])
    copies = fetch_factors(0, factors, factor, fsem)
    copy.wait()
    to_blocks(flat, hold)
    forward_blocks(copies, lambda g: hold[g], lambda g: hold[perms[0, g]], factor, out)
    fetch(out, out_h, sem.at[0]).wait()


def forward_mid(level, own_h, other_h, factors, out_h, own, other, factor, out, fsem, sem):
    moves = [fetch(own_h, own, sem.at[0]), fetch(other_h, other, sem.at[1])]
    copies = fetch_factors(level, factors, factor, fsem)
    for move in moves:
        move.wait()
    forward_blocks(copies, lambda g: own[g], lambda g: other[g], factor, out)
    fetch(out, out_h, sem.at[0]).wait()


def forward_split(level, place, own_h, other_h, factors, *rest):
    pieces, (own, other, factor, out, fsem, sem) = rest[:4], rest[4:]
    moves = [fetch(own_h, own, sem.at[0]), fetch(other_h, other, sem.at[1])]
    copies = fetch_factors(level, factors, factor, fsem)
    for move in moves:
        move.wait()
    forward_blocks(copies, lambda g: own[g], lambda g: other[g], factor, out)
    send_pieces(place[0], out, pieces, sem)


def forward_tail(place, perms, p0, p1, p2, p3, factors, out_h, hold, factor, out, flat, fsem, sem):
    moves = fetch_pieces(place[0], (p0, p1, p2, p3), hold, sem)
    copies = [fetch_factors(6 + n, factors, factor.at[n], fsem.at[n]) for n in range(3)]
    for move in moves:
        move.wait()
    forward_blocks(copies[0], lambda g: hold[g], lambda g: hold[g ^ WIDTH], factor.at[0], out)
    forward_blocks(copies[1], lambda g: out[g], lambda g: out[g ^ 2 * WIDTH], factor.at[1], hold)
    forward_blocks(copies[2], lambda g: hold[g], lambda g: hold[perms[1, g]], factor.at[2], out)
    for k in range(BLK // 16):
        part = slice(k * 16, k * 16 + 16)
        flat[part, :] = out[part].reshape(16, ROWS * LANES)
    fetch(flat, out_h, sem.at[0]).wait()


def adjoint_head(place, perms, source, factors, *rest):
    pieces, (flat, state, own, terms, factor, fsem, sem) = rest[:4], rest[4:]
    copy = fetch(source, flat, sem.at[0])
    copies = [fetch_factors(8 - n, factors, factor.at[n], fsem.at[n]) for n in range(3)]
    copy.wait()
    to_blocks(flat, state)
    low = low_half()

    def put(where, slot):
        def store(g, mine, parts):
            own[slot, g] = mine
            terms[slot, where(g)] = pack_terms(low, parts)

        return store

    def total(slot):
        return lambda g: (own[slot, g] + terms[slot, g]).astype(bf16)

    adjoint_blocks(copies[0], lambda g: state[g], factor.at[0], put(lambda g: perms[1, g], 0))
    adjoint_blocks(copies[1], total(0), factor.at[1], put(lambda g: g ^ 2 * WIDTH, 1))
    adjoint_blocks(copies[2], total(1), factor.at[2], put(lambda g: g ^ WIDTH, 0))
    for g in range(BLK):
        state[g] = total(0)(g)
    send_pieces(place[0], state, pieces, sem)


def adjoint_first(level, place, p0, p1, p2, p3, factors, own_h, terms_h, state, factor, own, terms, fsem, sem):
    moves = fetch_pieces(place[0], (p0, p1, p2, p3), state, sem)
    copies = fetch_factors(level, factors, factor, fsem)
    for move in moves:
        move.wait()
    low = low_half()

    def put(g, mine, parts):
        own[g] = mine
        terms[g] = pack_terms(low, [x.astype(bf16) for x in parts])

    adjoint_blocks(copies, lambda g: state[g], factor, put)
    moves = [fetch(terms, terms_h, sem.at[0]), fetch(own, own_h, sem.at[1])]
    for move in moves:
        move.wait()


def adjoint_mid(level, prev_h, back_h, factors, own_h, terms_h, prev, back, factor, own, terms, fsem, sem):
    moves = [fetch(prev_h, prev, sem.at[0]), fetch(back_h, back, sem.at[1])]
    copies = fetch_factors(level, factors, factor, fsem)
    for move in moves:
        move.wait()
    low = low_half()

    def put(g, mine, parts):
        own[g] = mine
        terms[g] = pack_terms(low, [x.astype(bf16) for x in parts])

    adjoint_blocks(copies, lambda g: (prev[g] + back[g].astype(f32)).astype(bf16), factor, put)
    moves = [fetch(terms, terms_h, sem.at[0]), fetch(own, own_h, sem.at[1])]
    for move in moves:
        move.wait()


def adjoint_tail(perms, prev_h, back_h, factors, out_h, prev, back, factor, own, terms, flat, fsem, sem):
    moves = [fetch(prev_h, prev, sem.at[0]), fetch(back_h, back, sem.at[1])]
    copies = fetch_factors(0, factors, factor, fsem)
    for move in moves:
        move.wait()
    low = low_half()

    def put(g, mine, parts):
        own[g] = mine
        terms[perms[0, g]] = pack_terms(low, parts)

    adjoint_blocks(copies, lambda g: (prev[g] + back[g].astype(f32)).astype(bf16), factor, put)
    for k in range(BLK // 16):
        part = slice(k * 16, k * 16 + 16)
        flat[part, :] = (own[part] + terms[part]).astype(bf16).reshape(16, ROWS * LANES)
    fetch(flat, out_h, sem.at[0]).wait()


FACTOR = (BLK, RANK, LANES)


def call(kernel, name, in_specs, outs, scratch, levels=1):
    return pl.pallas_call(
        kernel,
        name=name,
        in_specs=in_specs,
        out_specs=[HBM] * len(outs),
        out_shape=[jax.ShapeDtypeStruct(shape, kind) for shape, kind in outs],
        scratch_shapes=[pltpu.VMEM(shape, kind) for shape, kind in scratch]
        + [DMA((CHUNKS,) if levels == 1 else (levels, CHUNKS)), DMA((4,))],
        compiler_params=pltpu.CompilerParams(vmem_limit_bytes=48 * 2**20),
        cost_estimate=pl.CostEstimate(
            flops=levels * 2_000_000_000, bytes_accessed=levels * 3_000_000, transcendentals=0
        ),
    )


def from_partner(block, apart):
    count = lax.axis_size("pts")
    return lax.ppermute(block, "pts", [(n, n ^ (1 << apart)) for n in range(count)])


def reorder(pieces):
    count = lax.axis_size("lvl")
    return [pieces[0]] + [
        lax.ppermute(pieces[d], "lvl", [(n, n ^ d) for n in range(count)]) for d in range(1, 4)
    ]


def on_device(signal, adjoint_in, factors, perms):
    factors = jnp.swapaxes(factors, 2, 3)
    place = lax.axis_index("lvl").astype(jnp.int32).reshape(1)
    flat = (BLK, ROWS * LANES)
    state, wide = (STATE, bf16), (STATE, f32)
    hold, pieces = (FACTOR, bf16), [(PIECE, bf16)] * 4

    (ahead,) = call(
        forward_head, "fwd0", [SMEM, HBM, HBM], [state], [(flat, bf16), state, hold, state]
    )(perms, signal, factors)
    parts = call(
        adjoint_head,
        "adj876",
        [SMEM, SMEM, HBM, HBM],
        pieces,
        [(flat, bf16), state, ((2,) + STATE, f32), ((2,) + STATE, f32), ((3,) + FACTOR, bf16)],
        3,
    )(place, perms, adjoint_in, factors)
    parts = reorder(parts)
    for level in range(1, 5):
        other = from_partner(ahead, pair_bits[level - 1])
        (ahead,) = call(
            functools.partial(forward_mid, level), f"fwd{level}", [HBM] * 3, [state], [state, state, hold, state]
        )(ahead, other, factors)
    other = from_partner(ahead, pair_bits[4])
    ahead = call(
        functools.partial(forward_split, 5), "fwd5", [SMEM] + [HBM] * 3, pieces, [state, state, hold, state]
    )(place, ahead, other, factors)

    own, terms = call(
        functools.partial(adjoint_first, 5), "adj5", [SMEM] + [HBM] * 5, [wide, state], [state, hold, wide, state]
    )(place, *parts, factors)
    for level in range(4, 0, -1):
        back = from_partner(terms, pair_bits[level])
        own, terms = call(
            functools.partial(adjoint_mid, level), f"adj{level}", [HBM] * 3, [wide, state], [wide, state, hold, wide, state]
        )(own, back, factors)
    back = from_partner(terms, pair_bits[0])
    (adjoint_out,) = call(
        adjoint_tail, "adj0", [SMEM] + [HBM] * 3, [(flat, bf16)], [wide, state, hold, wide, wide, (flat, bf16)]
    )(perms, own, back, factors)
    ahead = reorder(ahead)
    (forward_out,) = call(
        forward_tail,
        "fwd678",
        [SMEM, SMEM] + [HBM] * 5,
        [(flat, bf16)],
        [state, ((3,) + FACTOR, bf16), state, (flat, bf16)],
        3,
    )(place, perms, *ahead, factors)
    return forward_out, adjoint_out


def solution(mesh):
    return jax.shard_map(
        on_device,
        mesh=mesh,
        in_specs=(
            P(("pts", "lvl"), None),
            P(("pts", "lvl"), None),
            P(None, ("pts", "lvl"), None, None),
            P(),
        ),
        out_specs=(P(("pts", "lvl"), None), P(("pts", "lvl"), None)),
        check_vma=False,
    )
```

```python
import functools

import jax
import jax.numpy as jnp
from jax import lax
from jax.experimental import pallas as pl
from jax.experimental.pallas import tpu as pltpu
from jax.sharding import PartitionSpec as P

f32, bf16 = jnp.float32, jnp.bfloat16
pair_bits = (0, 1, 2, 1, 0)
BLK, ROWS, LANES, RANK = 128, 16, 128, 64
CHUNKS, WIDTH = 4, 32
STATE = (BLK, ROWS, LANES)
PIECE = (WIDTH, ROWS, LANES)
NT = (((1,), (1,)), ((), ()))
NN = (((1,), (0,)), ((), ()))
HBM = pl.BlockSpec(memory_space=pl.ANY)
VMEM = pl.BlockSpec(memory_space=pltpu.VMEM)
SMEM = pl.BlockSpec(memory_space=pltpu.SMEM)
DMA = pltpu.SemaphoreType.DMA


def low_half():
    return lax.broadcasted_iota(jnp.int32, (ROWS, LANES), 1) < RANK


def swap(x):
    return jnp.concatenate([x[:, RANK:], x[:, :RANK]], 1)


def forward_pair(low, first, second, factor):
    rows = []
    for own, other in (first, second):
        rows += [jnp.where(low, own, swap(other)), jnp.where(low, swap(own), other)]
    out = lax.dot_general(
        jnp.concatenate(rows, 0), factor.reshape(2 * RANK, LANES), NT, preferred_element_type=f32
    ).astype(bf16)
    return (
        jnp.where(low, out[0:16], swap(out[16:32])),
        jnp.where(low, swap(out[32:48]), out[48:64]),
    )


def adjoint_pair(low, first, second, factor):
    zero = jnp.zeros((ROWS, LANES), bf16)
    rows = [
        jnp.where(low, first, zero),
        jnp.where(low, swap(first), zero),
        jnp.where(low, zero, swap(second)),
        jnp.where(low, zero, second),
    ]
    out = lax.dot_general(
        jnp.concatenate(rows, 0), factor.reshape(2 * RANK, LANES), NN, preferred_element_type=f32
    )
    return (out[0:16], out[16:32]), (out[32:48], out[48:64])


def pack_own(low, parts):
    return jnp.where(low, parts[0], swap(parts[1]))


def pack_terms(low, parts):
    return jnp.where(low, swap(parts[0]), parts[1])


def fetch_factors(level, factors, hold, sem):
    def copy(c):
        part = pl.ds(c * WIDTH, WIDTH)
        return pltpu.make_async_copy(factors.at[level, part], hold.at[part], sem.at[c])

    for c in range(CHUNKS):
        copy(c).start()
    return copy


def fetch(source, hold, sem):
    copy = pltpu.make_async_copy(source, hold, sem)
    copy.start()
    return copy


def fetch_pieces(place, pieces, hold, sem):
    return [
        fetch(piece, hold.at[pl.ds((place ^ d) * WIDTH, WIDTH)], sem.at[d])
        for d, piece in enumerate(pieces)
    ]


def send_pieces(place, hold, pieces, sem):
    copies = [
        fetch(hold.at[pl.ds((place ^ d) * WIDTH, WIDTH)], piece, sem.at[d])
        for d, piece in enumerate(pieces)
    ]
    for copy in copies:
        copy.wait()


def to_blocks(flat, hold):
    for k in range(BLK // 16):
        part = slice(k * 16, k * 16 + 16)
        hold[part] = flat[part, :].reshape(16, ROWS, LANES)


def each_group(copies, body):
    if copies is not None:
        for c in range(CHUNKS):
            copies(c).wait()
    for a in range(0, BLK, 2):
        body(a)


def forward_blocks(copies, own, other, factor, out):
    low = low_half()

    def body(a):
        out[a], out[a + 1] = forward_pair(
            low, (own(a), other(a)), (own(a + 1), other(a + 1)), factor[pl.ds(a, 2)]
        )

    each_group(copies, body)


def adjoint_blocks(copies, state, factor, put):
    low = low_half()

    def body(a):
        pair = adjoint_pair(low, state(a), state(a + 1), factor[pl.ds(a, 2)])
        for b in range(2):
            put(a + b, pack_own(low, pair[b]), pair[b])

    each_group(copies, body)


def fetch_parts(parts, hold, sem, base=0):
    size = BLK // len(parts)
    return [
        fetch(part, hold.at[pl.ds(n * size, size)], sem.at[base + n]) for n, part in enumerate(parts)
    ]


def send_parts(hold, parts, sem, base=0):
    size = BLK // len(parts)
    return [
        fetch(hold.at[pl.ds(n * size, size)], part, sem.at[base + n]) for n, part in enumerate(parts)
    ]


def wait_all(moves):
    for move in moves:
        move.wait()


def forward_head(perms, signal, factors, *rest):
    (ready, *outs), (flat, hold, factor, out, fsem, sem) = rest[:-6], rest[-6:]
    copy = fetch(signal, flat, sem.at[0])
    copies = fetch_factors(0, factors, factor, fsem)
    ahead = fetch(factors.at[1], ready, sem.at[7])
    copy.wait()
    to_blocks(flat, hold)
    forward_blocks(copies, lambda g: hold[g], lambda g: hold[perms[0, g]], factor, out)
    wait_all(send_parts(out, outs, sem) + [ahead])


def forward_mid(parts, *rest):
    owns, others, factors = rest[:parts], rest[parts : 2 * parts], rest[2 * parts]
    outs, (own, other, out, fsem, sem) = rest[2 * parts + 1 : -5], rest[-5:]
    moves = fetch_parts(owns, own, sem) + fetch_parts(others, other, sem, 4)
    wait_all(moves)
    forward_blocks(None, lambda g: own[g], lambda g: other[g], factors, out)
    wait_all(send_parts(out, outs, sem))


def forward_split(parts, place, *rest):
    owns, others, factors = rest[:parts], rest[parts : 2 * parts], rest[2 * parts]
    pieces, (own, other, out, fsem, sem) = rest[2 * parts + 1 : -5], rest[-5:]
    moves = fetch_parts(owns, own, sem) + fetch_parts(others, other, sem, 4)
    wait_all(moves)
    forward_blocks(None, lambda g: own[g], lambda g: other[g], factors, out)
    send_pieces(place[0], out, pieces, sem)


def forward_span(place, p0, p1, p2, p3, sixth, seventh, out_h, hold, out, fsem, sem):
    moves = fetch_pieces(place[0], (p0, p1, p2, p3), hold, sem)
    wait_all(moves)
    forward_blocks(None, lambda g: hold[g], lambda g: hold[g ^ WIDTH], sixth, out)
    forward_blocks(None, lambda g: out[g], lambda g: out[g ^ 2 * WIDTH], seventh, hold)
    fetch(hold, out_h, sem.at[0]).wait()


def forward_last(perms, own_h, factor, out_h, hold, out, flat, fsem, sem):
    fetch(own_h, hold, sem.at[0]).wait()
    forward_blocks(None, lambda g: hold[g], lambda g: hold[perms[1, g]], factor, out)
    for k in range(BLK // 16):
        part = slice(k * 16, k * 16 + 16)
        flat[part, :] = out[part].reshape(16, ROWS * LANES)
    fetch(flat, out_h, sem.at[0]).wait()


def adjoint_head(place, perms, source, factors, *rest):
    ready, factor, pieces = rest[:5], rest[5:8], rest[8:12]
    flat, state, own, terms, fsem, sem = rest[12:]
    copy = fetch(source, flat, sem.at[0])
    copies = [fetch_factors(8 - n, factors, factor[n], fsem.at[n]) for n in range(3)]
    copy.wait()
    to_blocks(flat, state)
    low = low_half()

    def put(where, slot):
        def store(g, mine, parts):
            own[slot, g] = mine
            terms[slot, where(g)] = pack_terms(low, parts)

        return store

    def total(slot):
        return lambda g: (own[slot, g] + terms[slot, g]).astype(bf16)

    adjoint_blocks(copies[0], lambda g: state[g], factor[0], put(lambda g: perms[1, g], 0))
    ahead = [fetch(factors.at[n], to, sem.at[4 + k]) for k, (n, to) in enumerate(zip((2, 5, 4, 3, 0), ready))]
    adjoint_blocks(copies[1], total(0), factor[1], put(lambda g: g ^ 2 * WIDTH, 1))
    adjoint_blocks(copies[2], total(1), factor[2], put(lambda g: g ^ WIDTH, 0))
    for g in range(BLK):
        state[g] = total(0)(g)
    send_pieces(place[0], state, pieces, sem)
    wait_all(ahead)


def adjoint_first(place, p0, p1, p2, p3, factors, own_h, *rest):
    terms_h, (state, own, terms, fsem, sem) = rest[:-5], rest[-5:]
    moves = fetch_pieces(place[0], (p0, p1, p2, p3), state, sem)
    wait_all(moves)
    low = low_half()

    def put(g, mine, parts):
        own[g] = mine
        terms[g] = pack_terms(low, [x.astype(bf16) for x in parts])

    adjoint_blocks(None, lambda g: state[g], factors, put)
    wait_all(send_parts(terms, terms_h, sem) + [fetch(own, own_h, sem.at[4])])


def adjoint_mid(parts, prev_h, *rest):
    backs, factors, own_h = rest[:parts], rest[parts], rest[parts + 1]
    terms_h, (prev, back, own, terms, fsem, sem) = rest[parts + 2 : -6], rest[-6:]
    moves = fetch_parts(backs, back, sem) + [fetch(prev_h, prev, sem.at[4])]
    wait_all(moves)
    low = low_half()

    def put(g, mine, parts):
        own[g] = mine
        terms[g] = pack_terms(low, [x.astype(bf16) for x in parts])

    adjoint_blocks(None, lambda g: (prev[g] + back[g].astype(f32)).astype(bf16), factors, put)
    wait_all(send_parts(terms, terms_h, sem) + [fetch(own, own_h, sem.at[4])])


def adjoint_tail(parts, perms, prev_h, *rest):
    backs, factors, out_h = rest[:parts], rest[parts], rest[parts + 1]
    prev, back, own, terms, flat, fsem, sem = rest[parts + 2 :]
    moves = fetch_parts(backs, back, sem) + [fetch(prev_h, prev, sem.at[4])]
    wait_all(moves)
    low = low_half()

    def put(g, mine, parts):
        own[g] = mine
        terms[perms[0, g]] = pack_terms(low, parts)

    adjoint_blocks(None, lambda g: (prev[g] + back[g].astype(f32)).astype(bf16), factors, put)
    for k in range(BLK // 16):
        part = slice(k * 16, k * 16 + 16)
        flat[part, :] = (own[part] + terms[part]).astype(bf16).reshape(16, ROWS * LANES)
    fetch(flat, out_h, sem.at[0]).wait()


FACTOR = (BLK, RANK, LANES)


def call(kernel, name, in_specs, outs, scratch, levels=1, cost=1):
    return pl.pallas_call(
        kernel,
        name=name,
        in_specs=in_specs,
        out_specs=[VMEM if shape == FACTOR else HBM for shape, _ in outs],
        out_shape=[jax.ShapeDtypeStruct(shape, kind) for shape, kind in outs],
        scratch_shapes=[pltpu.VMEM(shape, kind) for shape, kind in scratch]
        + [DMA((CHUNKS,) if levels == 1 else (levels, CHUNKS)), DMA((9,))],
        compiler_params=pltpu.CompilerParams(vmem_limit_bytes=(40 if name == "fwd0" else 30) * 2**20),
        cost_estimate=pl.CostEstimate(
            flops=cost * 1_000_000, bytes_accessed=1000, transcendentals=0
        ),
    )


def from_partner(blocks, apart):
    count = lax.axis_size("pts")
    return [lax.ppermute(x, "pts", [(n, n ^ (1 << apart)) for n in range(count)]) for x in blocks]


def reorder(pieces):
    count = lax.axis_size("lvl")
    return [pieces[0]] + [
        lax.ppermute(pieces[d], "lvl", [(n, n ^ d) for n in range(count)]) for d in range(1, 4)
    ]


CORE_PARTS = 2
ORDER = ("f0", "f1", "a8", "f2", "a5", "a4", "f3", "a3", "f4", "f5", "a2", "f6", "a1", "f8", "a0")
COST = dict(f0=20000, f1=20000, f2=2000, f3=2000, f4=1, f5=1, f6=40000, f8=2000, a8=6000, a5=1, a4=1, a3=2000, a2=1, a1=2000, a0=2000)


def on_device(signal, adjoint_in, factors, perms):
    factors = jnp.swapaxes(factors, 2, 3)
    place = lax.axis_index("lvl").astype(jnp.int32).reshape(1)
    flat = (BLK, ROWS * LANES)
    state, wide = (STATE, bf16), (STATE, f32)
    hold, pieces = (FACTOR, bf16), [(PIECE, bf16)] * 4
    mid = [state, state, state]
    amid = [wide, state, wide, state]
    have = {}

    def kernel(step, body, name, in_specs, outs, scratch, args, levels=1):
        if "last" in have:
            args, _ = lax.optimization_barrier((args, have["last"]))
        out = call(body, name, in_specs, outs, scratch, levels, COST[step])(*args)
        have["last"] = out[-1]
        return out

    def split(apart):
        parts = CORE_PARTS if apart == 0 else 1
        return [((BLK // parts, ROWS, LANES), bf16)] * parts

    for step in ORDER:
        side, level = step[0], int(step[1])
        if step == "f0":
            v = kernel(
                step, forward_head, "fwd0", [SMEM, HBM, HBM], [hold] + split(pair_bits[0]),
                [(flat, bf16), state, hold, state], (perms, signal, factors),
            )
            first, *v = v
            have["v"] = (*v, *from_partner(v, pair_bits[0]))
        elif step == "f6":
            have["v"] = kernel(
                step, forward_span, "fwd67", [SMEM] + [HBM] * 4 + [VMEM] * 2, [state],
                [state, state], (place, *have["v"], sixth, seventh),
            )
        elif step == "f8":
            (forward_out,) = kernel(
                step, forward_last, "fwd8", [SMEM, HBM, VMEM], [(flat, bf16)],
                [state, state, (flat, bf16)], (perms, *have["v"], eighth),
            )
        elif side == "f":
            args = (*have["v"], first if level == 1 else middle[level - 2])
            specs = [HBM] * (len(args) - 1) + [VMEM]
            parts = len(args) // 2
            if level == 5:
                v = kernel(step, functools.partial(forward_split, parts), "fwd5", [SMEM] + specs, pieces, mid, (place, *args))
                have["v"] = reorder(v)
            else:
                v = kernel(step, functools.partial(forward_mid, parts), f"fwd{level}", specs, split(pair_bits[level]), mid, args)
                have["v"] = (*v, *from_partner(v, pair_bits[level]))
        elif step == "a8":
            w = kernel(
                step, adjoint_head, "adj876", [SMEM, SMEM, HBM, HBM], [hold] * 8 + pieces,
                [(flat, bf16), state, ((2,) + STATE, f32), ((2,) + STATE, f32)],
                (place, perms, adjoint_in, factors), 3,
            )
            second, fifth, fourth, third, zeroth, eighth, seventh, sixth, *w = w
            middle = (second, third, fourth, fifth)
            have["w"] = reorder(w)
        elif step == "a0":
            args = (*have["w"], zeroth)
            (adjoint_out,) = kernel(
                step, functools.partial(adjoint_tail, len(args) - 2), "adj0", [SMEM] + [HBM] * (len(args) - 1) + [VMEM], [(flat, bf16)],
                [wide, state, wide, wide, (flat, bf16)], (perms, *args),
            )
        else:
            args = (*have["w"], first if level == 1 else middle[level - 2])
            outs = [wide] + split(pair_bits[level - 1])
            if level == 5:
                own, *terms = kernel(step, adjoint_first, "adj5", [SMEM] + [HBM] * 4 + [VMEM], outs, [state, wide, state], (place, *args))
            else:
                own, *terms = kernel(step, functools.partial(adjoint_mid, len(args) - 2), f"adj{level}", [HBM] * (len(args) - 1) + [VMEM], outs, amid, args)
            have["w"] = (own, *from_partner(terms, pair_bits[level - 1]))
    return forward_out, adjoint_out


def solution(mesh):
    return jax.shard_map(
        on_device,
        mesh=mesh,
        in_specs=(
            P(("pts", "lvl"), None),
            P(("pts", "lvl"), None),
            P(None, ("pts", "lvl"), None, None),
            P(),
        ),
        out_specs=(P(("pts", "lvl"), None), P(("pts", "lvl"), None)),
        check_vma=False,
    )
```

```python
import functools

import jax
import jax.numpy as jnp
from jax import lax
from jax.experimental import pallas as pl
from jax.experimental.pallas import tpu as pltpu
from jax.sharding import PartitionSpec as P

f32, bf16 = jnp.float32, jnp.bfloat16
pair_bits = (0, 1, 2, 1, 0)
BLK, ROWS, LANES, RANK = 128, 16, 128, 64
CHUNKS, WIDTH = 4, 32
STATE = (BLK, ROWS, LANES)
PIECE = (WIDTH, ROWS, LANES)
NT = (((1,), (1,)), ((), ()))
NN = (((1,), (0,)), ((), ()))
HBM = pl.BlockSpec(memory_space=pl.ANY)
VMEM = pl.BlockSpec(memory_space=pltpu.VMEM)
SMEM = pl.BlockSpec(memory_space=pltpu.SMEM)
DMA = pltpu.SemaphoreType.DMA


def low_half():
    return lax.broadcasted_iota(jnp.int32, (ROWS, LANES), 1) < RANK


def swap(x):
    return jnp.concatenate([x[:, RANK:], x[:, :RANK]], 1)


def forward_pair(low, first, second, factor):
    rows = []
    for own, other in (first, second):
        rows += [jnp.where(low, own, swap(other)), jnp.where(low, swap(own), other)]
    out = lax.dot_general(
        jnp.concatenate(rows, 0), factor.reshape(2 * RANK, LANES), NT, preferred_element_type=f32
    ).astype(bf16)
    return (
        jnp.where(low, out[0:16], swap(out[16:32])),
        jnp.where(low, swap(out[32:48]), out[48:64]),
    )


def adjoint_pair(low, first, second, factor):
    zero = jnp.zeros((ROWS, LANES), bf16)
    rows = [
        jnp.where(low, first, zero),
        jnp.where(low, swap(first), zero),
        jnp.where(low, zero, swap(second)),
        jnp.where(low, zero, second),
    ]
    out = lax.dot_general(
        jnp.concatenate(rows, 0), factor.reshape(2 * RANK, LANES), NN, preferred_element_type=f32
    )
    return (out[0:16], out[16:32]), (out[32:48], out[48:64])


def pack_own(low, parts):
    return jnp.where(low, parts[0], swap(parts[1]))


def pack_terms(low, parts):
    return jnp.where(low, swap(parts[0]), parts[1])


def fetch_factors(level, factors, hold, sem):
    def copy(c):
        part = pl.ds(c * WIDTH, WIDTH)
        return pltpu.make_async_copy(factors.at[level, part], hold.at[part], sem.at[c])

    for c in range(CHUNKS):
        copy(c).start()
    return copy


def fetch(source, hold, sem):
    copy = pltpu.make_async_copy(source, hold, sem)
    copy.start()
    return copy


def fetch_pieces(place, pieces, hold, sem):
    return [
        fetch(piece, hold.at[pl.ds((place ^ d) * WIDTH, WIDTH)], sem.at[d])
        for d, piece in enumerate(pieces)
    ]


def send_pieces(place, hold, pieces, sem):
    copies = [
        fetch(hold.at[pl.ds((place ^ d) * WIDTH, WIDTH)], piece, sem.at[d])
        for d, piece in enumerate(pieces)
    ]
    for copy in copies:
        copy.wait()


def to_blocks(flat, hold):
    for k in range(BLK // 16):
        part = slice(k * 16, k * 16 + 16)
        hold[part] = flat[part, :].reshape(16, ROWS, LANES)


def each_group(copies, body):
    if copies is not None:
        for c in range(CHUNKS):
            copies(c).wait()
    for a in range(0, BLK, 2):
        body(a)


def forward_blocks(copies, own, other, factor, out):
    low = low_half()

    def body(a):
        out[a], out[a + 1] = forward_pair(
            low, (own(a), other(a)), (own(a + 1), other(a + 1)), factor[pl.ds(a, 2)]
        )

    each_group(copies, body)


def adjoint_blocks(copies, state, factor, put):
    low = low_half()

    def body(a):
        pair = adjoint_pair(low, state(a), state(a + 1), factor[pl.ds(a, 2)])
        for b in range(2):
            put(a + b, pack_own(low, pair[b]), pair[b])

    each_group(copies, body)


def fetch_parts(parts, hold, sem, base=0):
    size = BLK // len(parts)
    return [
        fetch(part, hold.at[pl.ds(n * size, size)], sem.at[base + n]) for n, part in enumerate(parts)
    ]


def send_parts(hold, parts, sem, base=0):
    size = BLK // len(parts)
    return [
        fetch(hold.at[pl.ds(n * size, size)], part, sem.at[base + n]) for n, part in enumerate(parts)
    ]


def wait_all(moves):
    for move in moves:
        move.wait()


def forward_head(perms, signal, factors, *rest):
    (ready, *outs), (flat, hold, factor, out, fsem, sem) = rest[:-6], rest[-6:]
    copy = fetch(signal, flat, sem.at[0])
    copies = fetch_factors(0, factors, factor, fsem)
    ahead = fetch(factors.at[1], ready, sem.at[7])
    copy.wait()
    to_blocks(flat, hold)
    forward_blocks(copies, lambda g: hold[g], lambda g: hold[perms[0, g]], factor, out)
    wait_all(send_parts(out, outs, sem) + [ahead])


def forward_mid(parts, *rest):
    owns, others, factors = rest[:parts], rest[parts : 2 * parts], rest[2 * parts]
    outs, (own, other, out, fsem, sem) = rest[2 * parts + 1 : -5], rest[-5:]
    moves = fetch_parts(owns, own, sem) + fetch_parts(others, other, sem, 4)
    wait_all(moves)
    forward_blocks(None, lambda g: own[g], lambda g: other[g], factors, out)
    wait_all(send_parts(out, outs, sem))


def forward_split(parts, place, *rest):
    owns, others, factors = rest[:parts], rest[parts : 2 * parts], rest[2 * parts]
    pieces, (own, other, out, fsem, sem) = rest[2 * parts + 1 : -5], rest[-5:]
    moves = fetch_parts(owns, own, sem) + fetch_parts(others, other, sem, 4)
    wait_all(moves)
    forward_blocks(None, lambda g: own[g], lambda g: other[g], factors, out)
    send_pieces(place[0], out, pieces, sem)


def forward_span(place, p0, p1, p2, p3, sixth, seventh, out_h, hold, out, fsem, sem):
    moves = fetch_pieces(place[0], (p0, p1, p2, p3), hold, sem)
    wait_all(moves)
    forward_blocks(None, lambda g: hold[g], lambda g: hold[g ^ WIDTH], sixth, out)
    forward_blocks(None, lambda g: out[g], lambda g: out[g ^ 2 * WIDTH], seventh, hold)
    fetch(hold, out_h, sem.at[0]).wait()


def forward_last(perms, own_h, factor, out_h, hold, out, flat, fsem, sem):
    fetch(own_h, hold, sem.at[0]).wait()
    forward_blocks(None, lambda g: hold[g], lambda g: hold[perms[1, g]], factor, out)
    for k in range(BLK // 16):
        part = slice(k * 16, k * 16 + 16)
        flat[part, :] = out[part].reshape(16, ROWS * LANES)
    fetch(flat, out_h, sem.at[0]).wait()


def adjoint_head(place, perms, source, factors, *rest):
    ready, factor, pieces = rest[:5], rest[5:8], rest[8:12]
    flat, state, own, terms, fsem, sem = rest[12:]
    copy = fetch(source, flat, sem.at[0])
    copies = [fetch_factors(8 - n, factors, factor[n], fsem.at[n]) for n in range(3)]
    copy.wait()
    to_blocks(flat, state)
    low = low_half()

    def put(where, slot):
        def store(g, mine, parts):
            own[slot, g] = mine
            terms[slot, where(g)] = pack_terms(low, parts)

        return store

    def total(slot):
        return lambda g: (own[slot, g] + terms[slot, g]).astype(bf16)

    adjoint_blocks(copies[0], lambda g: state[g], factor[0], put(lambda g: perms[1, g], 0))
    ahead = [fetch(factors.at[n], to, sem.at[4 + k]) for k, (n, to) in enumerate(zip((2, 5, 4, 3, 0), ready))]
    adjoint_blocks(copies[1], total(0), factor[1], put(lambda g: g ^ 2 * WIDTH, 1))
    adjoint_blocks(copies[2], total(1), factor[2], put(lambda g: g ^ WIDTH, 0))
    for g in range(BLK):
        state[g] = total(0)(g)
    send_pieces(place[0], state, pieces, sem)
    wait_all(ahead)


def adjoint_first(place, p0, p1, p2, p3, factors, own_h, *rest):
    terms_h, (state, own, terms, fsem, sem) = rest[:-5], rest[-5:]
    moves = fetch_pieces(place[0], (p0, p1, p2, p3), state, sem)
    wait_all(moves)
    low = low_half()

    def put(g, mine, parts):
        own[g] = mine
        terms[g] = pack_terms(low, [x.astype(bf16) for x in parts])

    adjoint_blocks(None, lambda g: state[g], factors, put)
    wait_all(send_parts(terms, terms_h, sem) + [fetch(own, own_h, sem.at[4])])


def adjoint_mid(parts, prev_h, *rest):
    backs, factors, own_h = rest[:parts], rest[parts], rest[parts + 1]
    terms_h, (prev, back, own, terms, fsem, sem) = rest[parts + 2 : -6], rest[-6:]
    moves = fetch_parts(backs, back, sem) + [fetch(prev_h, prev, sem.at[4])]
    wait_all(moves)
    low = low_half()

    def put(g, mine, parts):
        own[g] = mine
        terms[g] = pack_terms(low, [x.astype(bf16) for x in parts])

    adjoint_blocks(None, lambda g: (prev[g] + back[g].astype(f32)).astype(bf16), factors, put)
    wait_all(send_parts(terms, terms_h, sem) + [fetch(own, own_h, sem.at[4])])


def adjoint_tail(parts, perms, prev_h, *rest):
    backs, factors, out_h = rest[:parts], rest[parts], rest[parts + 1]
    prev, back, own, terms, flat, fsem, sem = rest[parts + 2 :]
    moves = fetch_parts(backs, back, sem) + [fetch(prev_h, prev, sem.at[4])]
    wait_all(moves)
    low = low_half()

    def put(g, mine, parts):
        own[g] = mine
        terms[perms[0, g]] = pack_terms(low, parts)

    adjoint_blocks(None, lambda g: (prev[g] + back[g].astype(f32)).astype(bf16), factors, put)
    for k in range(BLK // 16):
        part = slice(k * 16, k * 16 + 16)
        flat[part, :] = (own[part] + terms[part]).astype(bf16).reshape(16, ROWS * LANES)
    fetch(flat, out_h, sem.at[0]).wait()


FACTOR = (BLK, RANK, LANES)


def call(kernel, name, in_specs, outs, scratch, levels=1, cost=1):
    return pl.pallas_call(
        kernel,
        name=name,
        in_specs=in_specs,
        out_specs=[VMEM if shape == FACTOR else HBM for shape, _ in outs],
        out_shape=[jax.ShapeDtypeStruct(shape, kind) for shape, kind in outs],
        scratch_shapes=[pltpu.VMEM(shape, kind) for shape, kind in scratch]
        + [DMA((CHUNKS,) if levels == 1 else (levels, CHUNKS)), DMA((9,))],
        compiler_params=pltpu.CompilerParams(vmem_limit_bytes=(40 if name == "fwd0" else 30) * 2**20),
        cost_estimate=pl.CostEstimate(
            flops=cost * 1_000_000, bytes_accessed=1000, transcendentals=0
        ),
    )


def from_partner(blocks, apart):
    count = lax.axis_size("pts")
    return [lax.ppermute(x, "pts", [(n, n ^ (1 << apart)) for n in range(count)]) for x in blocks]


def reorder(pieces):
    count = lax.axis_size("lvl")
    return [pieces[0]] + [
        lax.ppermute(pieces[d], "lvl", [(n, n ^ d) for n in range(count)]) for d in range(1, 4)
    ]


CORE_PARTS = 2
ORDER = ("f0", "f1", "a8", "f2", "a5", "a4", "f3", "a3", "f4", "f5", "a2", "f6", "f8", "a1", "a0")
COST = dict(f0=20000, f1=20000, f2=2000, f3=2000, f4=1, f5=1, f6=40000, f8=2000, a8=6000, a5=1, a4=1, a3=2000, a2=1, a1=2000, a0=2000)


def on_device(signal, adjoint_in, factors, perms):
    factors = jnp.swapaxes(factors, 2, 3)
    place = lax.axis_index("lvl").astype(jnp.int32).reshape(1)
    flat = (BLK, ROWS * LANES)
    state, wide = (STATE, bf16), (STATE, f32)
    hold, pieces = (FACTOR, bf16), [(PIECE, bf16)] * 4
    mid = [state, state, state]
    amid = [wide, state, wide, state]
    have = {}

    def kernel(step, body, name, in_specs, outs, scratch, args, levels=1):
        if "last" in have:
            args, _ = lax.optimization_barrier((args, have["last"]))
        out = call(body, name, in_specs, outs, scratch, levels, COST[step])(*args)
        have["last"] = out[-1]
        return out

    def split(apart):
        parts = CORE_PARTS if apart == 0 else 1
        return [((BLK // parts, ROWS, LANES), bf16)] * parts

    for step in ORDER:
        side, level = step[0], int(step[1])
        if step == "f0":
            v = kernel(
                step, forward_head, "fwd0", [SMEM, HBM, HBM], [hold] + split(pair_bits[0]),
                [(flat, bf16), state, hold, state], (perms, signal, factors),
            )
            first, *v = v
            have["v"] = (*v, *from_partner(v, pair_bits[0]))
        elif step == "f6":
            have["v"] = kernel(
                step, forward_span, "fwd67", [SMEM] + [HBM] * 4 + [VMEM] * 2, [state],
                [state, state], (place, *have["v"], sixth, seventh),
            )
        elif step == "f8":
            (forward_out,) = kernel(
                step, forward_last, "fwd8", [SMEM, HBM, VMEM], [(flat, bf16)],
                [state, state, (flat, bf16)], (perms, *have["v"], eighth),
            )
        elif side == "f":
            args = (*have["v"], first if level == 1 else middle[level - 2])
            specs = [HBM] * (len(args) - 1) + [VMEM]
            parts = len(args) // 2
            if level == 5:
                v = kernel(step, functools.partial(forward_split, parts), "fwd5", [SMEM] + specs, pieces, mid, (place, *args))
                have["v"] = reorder(v)
            else:
                v = kernel(step, functools.partial(forward_mid, parts), f"fwd{level}", specs, split(pair_bits[level]), mid, args)
                have["v"] = (*v, *from_partner(v, pair_bits[level]))
        elif step == "a8":
            w = kernel(
                step, adjoint_head, "adj876", [SMEM, SMEM, HBM, HBM], [hold] * 8 + pieces,
                [(flat, bf16), state, ((2,) + STATE, f32), ((2,) + STATE, f32)],
                (place, perms, adjoint_in, factors), 3,
            )
            second, fifth, fourth, third, zeroth, eighth, seventh, sixth, *w = w
            middle = (second, third, fourth, fifth)
            have["w"] = reorder(w)
        elif step == "a0":
            args = (*have["w"], zeroth)
            (adjoint_out,) = kernel(
                step, functools.partial(adjoint_tail, len(args) - 2), "adj0", [SMEM] + [HBM] * (len(args) - 1) + [VMEM], [(flat, bf16)],
                [wide, state, wide, wide, (flat, bf16)], (perms, *args),
            )
        else:
            args = (*have["w"], first if level == 1 else middle[level - 2])
            outs = [wide] + split(pair_bits[level - 1])
            if level == 5:
                own, *terms = kernel(step, adjoint_first, "adj5", [SMEM] + [HBM] * 4 + [VMEM], outs, [state, wide, state], (place, *args))
            else:
                own, *terms = kernel(step, functools.partial(adjoint_mid, len(args) - 2), f"adj{level}", [HBM] * (len(args) - 1) + [VMEM], outs, amid, args)
            have["w"] = (own, *from_partner(terms, pair_bits[level - 1]))
    return forward_out, adjoint_out


def solution(mesh):
    return jax.shard_map(
        on_device,
        mesh=mesh,
        in_specs=(
            P(("pts", "lvl"), None),
            P(("pts", "lvl"), None),
            P(None, ("pts", "lvl"), None, None),
            P(),
        ),
        out_specs=(P(("pts", "lvl"), None), P(("pts", "lvl"), None)),
        check_vma=False,
    )
```
